32 devices in a mesh: groups: 2 (over x), ctx: 16 (over z, y, core).
Axes of the slice: x: 2, y: 2, z: 4, core: 2. Of those that a mesh axis runs over, the one named last changes fastest.
Arguments:
- queries: bfloat16 [4096, 64, 128], P(('groups', 'ctx')), parts along dimension 0, may hold values from -5 to 5
- head_weights: float32 [4096, 64], P(('groups', 'ctx')), parts along dimension 0, may hold values from -2.5 to 2.5
- keys: bfloat16 [8192, 128], P(('groups', 'ctx')), parts along dimension 0, may hold values from -5 to 5
- targets: float32 [4096, 2048], P(('groups', 'ctx')), parts along dimension 0, may hold values from 0.001 to 1
- block_lists: int32 [64, 32], P(('groups', 'ctx')), parts along dimension 0, may hold values from -1 to 63, as said below
Outputs:
- grad_queries: bfloat16 [4096, 64, 128], P(('groups', 'ctx')), parts along dimension 0
- grad_weights: float32 [4096, 64], P(('groups', 'ctx')), parts along dimension 0
- grad_keys: bfloat16 [8192, 128], P(('groups', 'ctx')), parts along dimension 0
The draws below stay inside these ranges and needn't reach their ends.
There are 2 independent parts, one for each index of `groups`. The reference program is written for one: setup_inputs(seed, part) draws one part's arguments, and reference() takes and returns one part's arrays. A program takes and returns all parts, laid end to end along the dimension named above; each array names one. Nothing has to cross between parts.
Inputs may be any that keep to these rules, and one draw needn't show every extreme that they name: `block_lists`: row c names distinct blocks, none after b(c). Entry 0 is b(c), entries 1 and 2 are blocks 0 and 1; the named blocks come first and -1 fills the rest; some rows name 32 blocks. Over the 2 rows of one device, the blocks named from any one other device (a run of 4 blocks) number at most 2 distinct, blocks 0 and 1 included; every device other than the first reads exactly 2 from the first device.
All inputs are finite; a program needn't handle non-finite values.
Results may differ from the reference program's by a relative error of at most 0.0048.
Values may be sent and summed in bfloat16 or wider, within the bound.
A program may use at most 128 MiB of HBM per device.

```python
import math
import jax
import jax.numpy as jnp
from jax import lax

H = 64
DI = 128
BLK = 64
KSEL = 32
BLK_DEV = 4
QCH = 2
SEQ = 4096
BLOCKS = 64
Q_SPANS = 32
Q_TOKENS = 2048
CAP = 2


def base_keys(key):
    normal_key = jax.random.fold_in(key, 0)
    normal_part = jnp.clip(jax.random.normal(normal_key, (SEQ, DI), jnp.float32), -5.0, 5.0)
    return normal_part


def draw_keys(key, part):
    shared = base_keys(key)
    return shared.astype(jnp.bfloat16)


def draw_queries(key, part):
    key = jax.random.fold_in(key, 5)
    normal_key = jax.random.fold_in(key, 0)
    values = jnp.clip(jax.random.normal(normal_key, (Q_TOKENS, H, DI), jnp.float32), -5.0, 5.0)
    return values.astype(jnp.bfloat16)


def draw_head_weights(key, part):
    key = jax.random.fold_in(key, 7)
    first_key = jax.random.fold_in(key, 0)
    values = jnp.clip(0.5 * jax.random.normal(first_key, (Q_TOKENS, H), jnp.float32), -2.5, 2.5)
    return values


def draw_block_lists(key, part):
    key = jax.random.fold_in(key, 11)
    slot_key, score_key = jax.random.split(key)
    device_count = Q_SPANS // QCH
    noise = jax.random.randint(slot_key, (device_count, device_count, BLK_DEV), 0, 65536)
    ranked = noise * BLK_DEV + jnp.arange(BLK_DEV, dtype=jnp.int32)
    unused, picked = lax.top_k(ranked, CAP)
    holders = jnp.arange(device_count, dtype=jnp.int32)
    remote_blocks = (holders[None, :, None] * BLK_DEV + picked).reshape(device_count, device_count * CAP)
    remote_ok = (holders[None, :] >= 1) & (holders[None, :] < holders[:, None])
    remote_ok = jnp.broadcast_to(remote_ok[:, :, None], (device_count, device_count, CAP)).reshape(device_count, device_count * CAP)
    query_ids = jnp.arange(Q_SPANS, dtype=jnp.int32)
    device_of = query_ids // QCH
    own_block = device_of * BLK_DEV + BLK_DEV - QCH + query_ids % QCH
    local_blocks = device_of[:, None] * BLK_DEV + jnp.arange(BLK_DEV, dtype=jnp.int32)[None, :]
    local_ok = (local_blocks >= 2) & (local_blocks < own_block[:, None])
    pool = jnp.concatenate([remote_blocks[device_of], local_blocks], axis=1)
    pool_ok = jnp.concatenate([remote_ok[device_of], local_ok], axis=1)
    pool_size = pool.shape[1]
    scores = jax.random.randint(score_key, (Q_SPANS, pool_size), 0, 65536) * pool_size + jnp.arange(pool_size, dtype=jnp.int32)[None, :]
    scores = jnp.where(pool_ok, scores + 65536 * pool_size, scores)
    unused_top, order = lax.top_k(scores, KSEL - 3)
    chosen = jnp.take_along_axis(pool, order, axis=1)
    chosen_ok = jnp.take_along_axis(pool_ok, order, axis=1)
    tail = jnp.where(chosen_ok, chosen, -1)
    head = jnp.stack([own_block, jnp.zeros_like(own_block), jnp.ones_like(own_block)], axis=1)
    return jnp.concatenate([head, tail], axis=1).astype(jnp.int32)


def block_scale(stream_key, extent, cuts, least, top_value):
    level = 1.0
    for axis_at, shards_of in cuts:
        draws = jax.random.uniform(jax.random.fold_in(jax.random.fold_in(stream_key, 6), axis_at), (shards_of,), jnp.float32, least / len(cuts), top_value / len(cuts))
        level = level * jnp.repeat(jnp.exp(draws), extent[axis_at] // shards_of).reshape((-1,) + (1,) * (len(extent) - 1 - axis_at))
    return level


def setup_inputs(seed: int = 0, part: int = 0) -> dict:
    splits = jax.random.split(jax.random.key(seed), 6)
    part_splits = jax.random.split(jax.random.fold_in(splits[5], part), 6)
    return {
        "queries": draw_queries(jax.random.fold_in(jax.random.fold_in(splits[5], part), 71), part),
        "head_weights": draw_head_weights(jax.random.fold_in(jax.random.fold_in(splits[5], part), 71), part),
        "keys": draw_keys(jax.random.fold_in(jax.random.fold_in(splits[5], part), 71), part),
        "targets": jnp.clip(jnp.exp(math.log(1.0) - 6.9077552 * jax.random.uniform(part_splits[3], (Q_TOKENS, KSEL * BLK), jnp.float32) ** block_scale(part_splits[3], (Q_TOKENS, KSEL * BLK), ((0, 16),), -0.2, 0.2)), 0.001, 1.0),
        "block_lists": draw_block_lists(jax.random.fold_in(jax.random.fold_in(splits[5], part), 71), part),
    }


loss_weight = 256.0

def causal_mask(entries, own_block):
    usable = entries >= 0
    clamped = jnp.where(usable, entries, 0).astype(jnp.int32)
    offsets = jnp.arange(BLK, dtype=jnp.int32)
    key_pos = (clamped[:, None] * BLK + offsets[None, :]).reshape(-1)
    key_ok = jnp.broadcast_to(usable[:, None], (entries.shape[0], BLK)).reshape(-1)
    query_pos = own_block * BLK + offsets
    return key_ok[None, :] & (key_pos[None, :] <= query_pos[:, None])

def query_block_grads(queries, weights, key_rows, targets, allowed):
    row_count = queries.shape[0]
    head_count = queries.shape[1]
    key_count = key_rows.shape[0]
    key_width = key_rows.shape[1]
    block_width = min(512, key_count)
    groups = key_count // block_width
    inv_root = 1.0 / math.sqrt(key_width)
    key_groups = key_rows.reshape(groups, block_width, key_width)
    query_wide = queries.astype(jnp.float32)

    def scores(key_block):
        return jnp.einsum('thd,ud->thu', query_wide, key_block.astype(jnp.float32), precision=lax.Precision.HIGHEST) * inv_root

    def index_part(key_block):
        return lax.optimization_barrier(jnp.sum(weights[:, :, None] * jax.nn.relu(scores(key_block)), axis=1))
    index_score = lax.map(index_part, key_groups)
    index_score = jnp.transpose(index_score, (1, 0, 2)).reshape(row_count, key_count)
    logits = jnp.where(allowed, index_score, -jnp.inf)
    row_peak = lax.optimization_barrier(jnp.max(logits, axis=1, keepdims=True))
    raised = jnp.exp(logits - row_peak)
    predicted = raised / lax.optimization_barrier(jnp.sum(raised, axis=1, keepdims=True))
    masked = jnp.where(allowed, targets, 0.0)
    target_prob = masked / lax.optimization_barrier(jnp.sum(masked, axis=1, keepdims=True))
    logit_grad = (predicted - target_prob) * loss_weight
    grad_parts = jnp.transpose(logit_grad.reshape(row_count, groups, block_width), (1, 0, 2))

    def backward(running, pieces):
        key_block, grad_part = pieces
        grad_q, grad_w = running
        head_score = scores(key_block)
        grad_w = grad_w + lax.optimization_barrier(jnp.sum(grad_part[:, None, :] * jax.nn.relu(head_score), axis=2))
        mixed = jnp.where(head_score > 0, grad_part[:, None, :] * weights[:, :, None] * inv_root, 0.0).astype(jnp.bfloat16)
        mixed_wide = mixed.astype(jnp.float32)
        grad_q = grad_q + jnp.einsum('thu,ud->thd', mixed_wide, key_block.astype(jnp.float32), precision=lax.Precision.HIGHEST)
        grad_k = jnp.einsum('thu,thd->ud', mixed_wide, query_wide, precision=lax.Precision.HIGHEST)
        return ((grad_q, grad_w), grad_k)
    start_state = (jnp.zeros((row_count, head_count, key_width), jnp.float32), jnp.zeros((row_count, head_count), jnp.float32))
    (grad_q, grad_w), grad_k = lax.scan(backward, start_state, (key_groups, grad_parts))
    return (grad_q.astype(jnp.bfloat16), grad_w, grad_k.reshape(key_count, key_width))

def reference(queries, head_weights, keys, targets, block_lists):
    key_table = keys.reshape(BLOCKS, BLK, DI)

    def per_block(grad_table, inputs_now):
        query_rows, weight_rows, target_rows, entries, block_id = inputs_now
        own_block = block_id // QCH * BLK_DEV + BLK_DEV - QCH + block_id % QCH
        clamped = jnp.where(entries >= 0, entries, 0).astype(jnp.int32)
        key_rows = key_table[clamped].reshape(KSEL * BLK, DI)
        allowed = causal_mask(entries, own_block)
        grad_q, grad_w, grad_k = query_block_grads(query_rows, weight_rows, key_rows, target_rows, allowed)
        grad_table = grad_table.at[clamped].add(grad_k.reshape(KSEL, BLK, DI))
        return (grad_table, (grad_q, grad_w))
    inputs_all = (queries.reshape(Q_SPANS, BLK, H, DI), head_weights.reshape(Q_SPANS, BLK, H), targets.reshape(Q_SPANS, BLK, KSEL * BLK), block_lists, jnp.arange(Q_SPANS, dtype=jnp.int32))
    grad_table, (grad_q, grad_w) = lax.scan(per_block, jnp.zeros((BLOCKS, BLK, DI), jnp.float32), inputs_all)
    return (grad_q.reshape(Q_TOKENS, H, DI), grad_w.reshape(Q_TOKENS, H), grad_table.reshape(SEQ, DI).astype(jnp.bfloat16))
```

```python
import functools
import math

import jax
import jax.numpy as jnp
from jax import lax
from jax.experimental import pallas as pl
from jax.experimental.pallas import tpu as pltpu
from jax.sharding import PartitionSpec as P

BLK = 64
LOSS_WEIGHT = 256.0
FAR = 2**30
UC = 256
TF = 8
TB = 8


def compute_kernel(
    lists, q_ref, w_ref, table_ref, targets_ref, gq_ref, gw_ref, gk_ref,
    k_scr, kt_scr, s_scr, wb_scr, idx_scr, g_scr, gkt_scr,
):
    c = pl.program_id(0)
    tokens, heads, width = q_ref.shape
    cand = targets_ref.shape[1]
    entries = cand // BLK
    inv_root = 1.0 / math.sqrt(width)

    @pl.when(c == 0)
    def _():
        gk_ref[...] = jnp.zeros_like(gk_ref)

    for e in range(entries):
        source = jnp.maximum(lists[c, e], 0)
        k_scr[e * BLK : (e + 1) * BLK, :] = table_ref[source]
    kt_scr[...] = k_scr[...].T
    gkt_scr[...] = jnp.zeros_like(gkt_scr)

    for t0 in range(0, tokens, 8):
        wb_scr[t0 : t0 + 8] = jnp.broadcast_to(
            (w_ref[t0 : t0 + 8, :] * inv_root)[:, :, None], (8, heads, width)
        )

    def forward(i, carry):
        t0 = pl.multiple_of(i * TF, TF)
        q = q_ref[pl.ds(t0, TF)].reshape(TF * heads, width)
        for u in range(0, cand, UC):
            s = jnp.dot(q, kt_scr[:, u : u + UC], preferred_element_type=jnp.float32)
            s_scr[pl.ds(t0 * heads, TF * heads), u : u + UC] = s.astype(jnp.bfloat16)
            s = jnp.maximum(s, 0.0).reshape(TF, heads, UC)
            parts = [
                jnp.sum(wb_scr[pl.ds(t0, TF)] * s[:, :, v : v + width], axis=1)
                for v in range(0, UC, width)
            ]
            idx_scr[pl.ds(t0, TF), u : u + UC] = jnp.concatenate(parts, axis=1)
        return carry

    lax.fori_loop(0, tokens // TF, forward, 0)

    lane = lax.broadcasted_iota(jnp.int32, (1, 2 * BLK), 1)
    pieces = []
    for e in range(0, entries, 2):
        low = jnp.where(lists[c, e] >= 0, lists[c, e] * BLK, FAR)
        high = jnp.where(lists[c, e + 1] >= 0, lists[c, e + 1] * BLK - BLK, FAR)
        pieces.append(jnp.where(lane < BLK, low, high) + lane)
    key_pos = jnp.concatenate(pieces, axis=1)
    for t0 in range(0, tokens, 8):
        row = lax.broadcasted_iota(jnp.int32, (8, cand), 0) + (lists[c, 0] * BLK + t0)
        allowed = key_pos <= row
        logits = jnp.where(allowed, idx_scr[t0 : t0 + 8, :], -jnp.inf)
        peak = jnp.max(logits, axis=1, keepdims=True)
        raised = jnp.exp(logits - peak)
        masked = jnp.where(allowed, targets_ref[t0 : t0 + 8, :], 0.0)
        p_scale = LOSS_WEIGHT / jnp.sum(raised, axis=1, keepdims=True)
        t_scale = LOSS_WEIGHT / jnp.sum(masked, axis=1, keepdims=True)
        g_scr[t0 : t0 + 8, :] = raised * p_scale - masked * t_scale

    def backward(i, carry):
        t0 = pl.multiple_of(i * TB, TB)
        rows = TB * heads
        q = q_ref[pl.ds(t0, TB)].astype(jnp.float32)
        wb = wb_scr[pl.ds(t0, TB)]
        wqt = (q * wb).reshape(rows, width).T.astype(jnp.bfloat16)
        gq = jnp.zeros((rows, width), jnp.float32)
        for u in range(0, cand, UC):
            g = g_scr[pl.ds(t0, TB), u : u + UC]
            g = jnp.broadcast_to(g[:, None, :], (TB, 16, UC)).astype(jnp.bfloat16)
            s = s_scr[pl.ds(t0 * heads, rows), u : u + UC].reshape(TB, heads // 16, 16, UC)
            mixed = jnp.where(s > 0, g[:, None], jnp.zeros((), jnp.bfloat16)).reshape(rows, UC)
            gq = gq + jnp.dot(
                mixed, k_scr[u : u + UC, :], preferred_element_type=jnp.float32
            )
            gkt_scr[:, u : u + UC] += jnp.dot(
                wqt, mixed, preferred_element_type=jnp.float32
            )
        gq = gq.reshape(TB, heads, width)
        gq_ref[pl.ds(t0, TB)] = (gq * wb).astype(jnp.bfloat16)
        gw_ref[pl.ds(t0, TB), :] = jnp.sum(gq * q, axis=2) * inv_root
        return carry

    lax.fori_loop(0, tokens // TB, backward, 0)

    for u in range(0, cand, 2 * BLK):
        part = gkt_scr[:, u : u + 2 * BLK].T
        for v in range(2):
            target = jnp.maximum(lists[c, u // BLK + v], 0)
            gk_ref[target] += part[v * BLK : (v + 1) * BLK, :]


def shards(queries, head_weights, keys, targets, block_lists):
    width = keys.shape[1]
    heads = queries.shape[1]
    cand = targets.shape[1]
    blocks_here = block_lists.shape[0]
    everyone = lax.all_gather(keys, "ctx", axis=0, tiled=True)
    total = everyone.shape[0] // BLK
    table = everyone.reshape(total, BLK, width)
    flops = 6 * queries.shape[0] * heads * cand * width
    once = pl.Buffered(1)
    grad_q, grad_w, grad_table = pl.pallas_call(
        compute_kernel,
        grid_spec=pltpu.PrefetchScalarGridSpec(
            num_scalar_prefetch=1,
            grid=(blocks_here,),
            in_specs=[
                pl.BlockSpec((BLK, heads, width), lambda c, lists: (c, 0, 0)),
                pl.BlockSpec((BLK, heads), lambda c, lists: (c, 0)),
                pl.BlockSpec((total, BLK, width), lambda c, lists: (0, 0, 0), pipeline_mode=once),
                pl.BlockSpec((BLK, cand), lambda c, lists: (c, 0)),
            ],
            out_specs=[
                pl.BlockSpec((BLK, heads, width), lambda c, lists: (c, 0, 0)),
                pl.BlockSpec((BLK, heads), lambda c, lists: (c, 0)),
                pl.BlockSpec((total, BLK, width), lambda c, lists: (0, 0, 0), pipeline_mode=once),
            ],
            scratch_shapes=[
                pltpu.VMEM((cand, width), jnp.bfloat16),
                pltpu.VMEM((width, cand), jnp.bfloat16),
                pltpu.VMEM((BLK * heads, cand), jnp.bfloat16),
                pltpu.VMEM((BLK, heads, width), jnp.float32),
                pltpu.VMEM((BLK, cand), jnp.float32),
                pltpu.VMEM((BLK, cand), jnp.float32),
                pltpu.VMEM((width, cand), jnp.float32),
            ],
        ),
        out_shape=[
            jax.ShapeDtypeStruct(queries.shape, jnp.bfloat16),
            jax.ShapeDtypeStruct(head_weights.shape, jnp.float32),
            jax.ShapeDtypeStruct((total, BLK, width), jnp.float32),
        ],
        compiler_params=pltpu.CompilerParams(vmem_limit_bytes=60 * 2**20),
        cost_estimate=pl.CostEstimate(flops=flops, bytes_accessed=10 * 2**20, transcendentals=0),
    )(block_lists, queries, head_weights, table, targets)
    summed = lax.psum_scatter(
        grad_table.reshape(-1, width), "ctx", scatter_dimension=0, tiled=True
    )
    return (grad_q, grad_w, summed.astype(jnp.bfloat16))


def solution(mesh):
    in_specs = (
        P(("groups", "ctx"), None, None),
        P(("groups", "ctx"), None),
        P(("groups", "ctx"), None),
        P(("groups", "ctx"), None),
        P(("groups", "ctx"), None),
    )
    out_specs = (
        P(("groups", "ctx"), None, None),
        P(("groups", "ctx"), None),
        P(("groups", "ctx"), None),
    )
    return jax.shard_map(shards, mesh=mesh, in_specs=in_specs, out_specs=out_specs, check_vma=False)
```

```python
import functools
import math

import jax
import jax.numpy as jnp
from jax import lax
from jax.experimental import pallas as pl
from jax.experimental.pallas import tpu as pltpu
from jax.sharding import PartitionSpec as P

BLK = 64
LOSS_WEIGHT = 256.0
FAR = 2**30
UC = 256
TF = 8
TB = 8


def compute_kernel(
    lists, q_ref, w_ref, table_ref, targets_ref, gq_ref, gw_ref, gk_ref,
    k_scr, kt_scr, s_scr, wb_scr, idx_scr, g_scr, gkt_scr,
):
    c = pl.program_id(0)
    tokens, heads, width = q_ref.shape
    cand = targets_ref.shape[1]
    entries = cand // BLK
    inv_root = 1.0 / math.sqrt(width)

    @pl.when(c == 0)
    def _():
        gk_ref[...] = jnp.zeros_like(gk_ref)

    for e in range(entries):
        source = jnp.maximum(lists[c, e], 0)
        k_scr[e * BLK : (e + 1) * BLK, :] = table_ref[source]
    kt_scr[...] = k_scr[...].T
    gkt_scr[...] = jnp.zeros_like(gkt_scr)

    for t0 in range(0, tokens, 8):
        wb_scr[t0 : t0 + 8] = jnp.broadcast_to(
            (w_ref[t0 : t0 + 8, :] * inv_root)[:, :, None], (8, heads, width)
        )

    def forward(i, carry):
        t0 = pl.multiple_of(i * TF, TF)
        q = q_ref[pl.ds(t0, TF)].reshape(TF * heads, width)
        for u in range(0, cand, UC):
            s = jnp.dot(q, kt_scr[:, u : u + UC], preferred_element_type=jnp.float32)
            s_scr[pl.ds(t0 * heads, TF * heads), u : u + UC] = s.astype(jnp.bfloat16)
            s = jnp.maximum(s, 0.0).reshape(TF, heads, UC)
            parts = [
                jnp.sum(wb_scr[pl.ds(t0, TF)] * s[:, :, v : v + width], axis=1)
                for v in range(0, UC, width)
            ]
            idx_scr[pl.ds(t0, TF), u : u + UC] = jnp.concatenate(parts, axis=1)
        return carry

    lax.fori_loop(0, tokens // TF, forward, 0)

    lane = lax.broadcasted_iota(jnp.int32, (1, 2 * BLK), 1)
    pieces = []
    for e in range(0, entries, 2):
        low = jnp.where(lists[c, e] >= 0, lists[c, e] * BLK, FAR)
        high = jnp.where(lists[c, e + 1] >= 0, lists[c, e + 1] * BLK - BLK, FAR)
        pieces.append(jnp.where(lane < BLK, low, high) + lane)
    key_pos = jnp.concatenate(pieces, axis=1)
    for t0 in range(0, tokens, 8):
        row = lax.broadcasted_iota(jnp.int32, (8, cand), 0) + (lists[c, 0] * BLK + t0)
        allowed = key_pos <= row
        logits = jnp.where(allowed, idx_scr[t0 : t0 + 8, :], -jnp.inf)
        peak = jnp.max(logits, axis=1, keepdims=True)
        raised = jnp.exp(logits - peak)
        masked = jnp.where(allowed, targets_ref[t0 : t0 + 8, :], 0.0)
        p_scale = LOSS_WEIGHT / jnp.sum(raised, axis=1, keepdims=True)
        t_scale = LOSS_WEIGHT / jnp.sum(masked, axis=1, keepdims=True)
        g_scr[t0 : t0 + 8, :] = raised * p_scale - masked * t_scale

    def backward(i, carry):
        t0 = pl.multiple_of(i * TB, TB)
        rows = TB * heads
        q = q_ref[pl.ds(t0, TB)].astype(jnp.float32)
        wb = wb_scr[pl.ds(t0, TB)]
        wqt = (q * wb).reshape(rows, width).T.astype(jnp.bfloat16)
        gq = jnp.zeros((rows, width), jnp.float32)
        for u in range(0, cand, UC):
            g = g_scr[pl.ds(t0, TB), u : u + UC]
            g = jnp.broadcast_to(g[:, None, :], (TB, 16, UC)).astype(jnp.bfloat16)
            s = s_scr[pl.ds(t0 * heads, rows), u : u + UC].reshape(TB, heads // 16, 16, UC)
            mixed = jnp.where(s > 0, g[:, None], jnp.zeros((), jnp.bfloat16)).reshape(rows, UC)
            gq = gq + jnp.dot(
                mixed, k_scr[u : u + UC, :], preferred_element_type=jnp.float32
            )
            gkt_scr[:, u : u + UC] += jnp.dot(
                wqt, mixed, preferred_element_type=jnp.float32
            )
        gq = gq.reshape(TB, heads, width)
        gq_ref[pl.ds(t0, TB)] = (gq * wb).astype(jnp.bfloat16)
        gw_ref[pl.ds(t0, TB), :] = jnp.sum(gq * q, axis=2) * inv_root
        return carry

    lax.fori_loop(0, tokens // TB, backward, 0)

    for u in range(0, cand, 2 * BLK):
        part = gkt_scr[:, u : u + 2 * BLK].T
        for v in range(2):
            target = jnp.maximum(lists[c, u // BLK + v], 0)
            gk_ref[target] += part[v * BLK : (v + 1) * BLK, :]


def axis_bits(count):
    return count.bit_length() - 1


def relative(me, r, bits):
    where = me
    for b in range(bits):
        if (r >> b) & 1:
            where = where + (1 - 2 * ((me // 2**b) % 2)) * 2**b
    return where


def low_bit(r, bits):
    return bits if r == 0 else (r & -r).bit_length() - 1


def greet(me, bits):
    barrier = pltpu.get_barrier_semaphore()
    for b in range(bits):
        pl.semaphore_signal(
            barrier,
            inc=1,
            device_id={"ctx": relative(me, 2**b, bits)},
            device_id_type=pl.DeviceIdType.MESH,
        )
    pl.semaphore_wait(barrier, bits)


def gather_kernel(count, keys_ref, all_ref, send_sem, recv_sem, own_sem):
    me = lax.axis_index("ctx")
    bits = axis_bits(count)
    own = pltpu.make_async_copy(keys_ref, all_ref.at[me], own_sem)
    own.start()
    greet(me, bits)

    def hop(r, b):
        where = relative(me, r, bits)
        return pltpu.make_async_remote_copy(
            src_ref=keys_ref if r == 0 else all_ref.at[where],
            dst_ref=all_ref.at[where],
            send_sem=send_sem.at[r + 2**b],
            recv_sem=recv_sem.at[r + 2**b],
            device_id={"ctx": relative(me, 2**b, bits)},
            device_id_type=pl.DeviceIdType.MESH,
        )

    def landed(r):
        where = relative(me, r, bits)
        return pltpu.make_async_remote_copy(
            src_ref=all_ref.at[where],
            dst_ref=all_ref.at[where],
            send_sem=send_sem.at[r],
            recv_sem=recv_sem.at[r],
            device_id={"ctx": relative(me, 2 ** low_bit(r, bits), bits)},
            device_id_type=pl.DeviceIdType.MESH,
        )

    sent = []
    for b in reversed(range(bits)):
        sent.append(hop(0, b))
        sent[-1].start()
    order = sorted(range(1, count), key=lambda r: (bin(r).count("1"), -low_bit(r, bits)))
    for r in order:
        landed(r).wait_recv()
        for b in reversed(range(low_bit(r, bits))):
            sent.append(hop(r, b))
            sent[-1].start()
    own.wait()
    for copy in sent:
        copy.wait_send()


def reduce_kernel(count, terms_ref, out_ref, send_buf, wide_buf, recv_buf, send_sem, recv_sem):
    me = lax.axis_index("ctx")
    bits = axis_bits(count)
    greet(me, bits)

    def hop(r):
        b = low_bit(r, bits)
        if b == 0:
            src, dst = terms_ref.at[relative(me, r, bits)], wide_buf.at[r // 2]
        else:
            src, dst = send_buf.at[r // 2], recv_buf.at[r // 2]
        return pltpu.make_async_remote_copy(
            src_ref=src,
            dst_ref=dst,
            send_sem=send_sem.at[r],
            recv_sem=recv_sem.at[r],
            device_id={"ctx": relative(me, 2**b, bits)},
            device_id_type=pl.DeviceIdType.MESH,
        )

    def total(r):
        value = terms_ref[relative(me, r, bits)]
        for b in range(low_bit(r, bits)):
            hop(r + 2**b).wait_recv()
            if b == 0:
                value = value + wide_buf[r // 2]
            else:
                value = value + recv_buf[(r + 2**b) // 2].astype(jnp.float32)
        return value

    def rank(r):
        b = low_bit(r, bits)
        return (b, low_bit(r - 2**b, bits), -r)

    order = sorted(range(1, count), key=rank)
    for r in order:
        if low_bit(r, bits) > 0:
            send_buf[r // 2] = total(r).astype(jnp.bfloat16)
        hop(r).start()
    out_ref[...] = total(0).astype(jnp.bfloat16)
    for r in order:
        hop(r).wait_send()


def gather_keys(keys):
    count = lax.axis_size("ctx")
    return pl.pallas_call(
        functools.partial(gather_kernel, count),
        out_shape=jax.ShapeDtypeStruct((count,) + keys.shape, keys.dtype),
        in_specs=[pl.BlockSpec(memory_space=pltpu.VMEM)],
        out_specs=pl.BlockSpec(memory_space=pltpu.VMEM),
        scratch_shapes=[
            pltpu.SemaphoreType.DMA((count,)),
            pltpu.SemaphoreType.DMA((count,)),
            pltpu.SemaphoreType.DMA,
        ],
        compiler_params=pltpu.CompilerParams(
            collective_id=0, has_side_effects=True, vmem_limit_bytes=32 * 2**20
        ),
    )(keys)


def reduce_terms(terms):
    count, rows, width = terms.shape
    return pl.pallas_call(
        functools.partial(reduce_kernel, count),
        out_shape=jax.ShapeDtypeStruct((rows, width), jnp.bfloat16),
        in_specs=[pl.BlockSpec(memory_space=pltpu.VMEM)],
        out_specs=pl.BlockSpec(memory_space=pltpu.VMEM),
        scratch_shapes=[
            pltpu.VMEM((count // 2, rows, width), jnp.bfloat16),
            pltpu.VMEM((count // 2, rows, width), jnp.float32),
            pltpu.VMEM((count // 2, rows, width), jnp.bfloat16),
            pltpu.SemaphoreType.DMA((count,)),
            pltpu.SemaphoreType.DMA((count,)),
        ],
        compiler_params=pltpu.CompilerParams(
            collective_id=1, has_side_effects=True, vmem_limit_bytes=52 * 2**20
        ),
    )(terms)


def shards(queries, head_weights, keys, targets, block_lists):
    width = keys.shape[1]
    heads = queries.shape[1]
    cand = targets.shape[1]
    blocks_here = block_lists.shape[0]
    everyone = gather_keys(keys)
    total = everyone.shape[0] * everyone.shape[1] // BLK
    table = everyone.reshape(total, BLK, width)
    flops = 6 * queries.shape[0] * heads * cand * width
    once = pl.Buffered(1)
    grad_q, grad_w, grad_table = pl.pallas_call(
        compute_kernel,
        grid_spec=pltpu.PrefetchScalarGridSpec(
            num_scalar_prefetch=1,
            grid=(blocks_here,),
            in_specs=[
                pl.BlockSpec((BLK, heads, width), lambda c, lists: (c, 0, 0)),
                pl.BlockSpec((BLK, heads), lambda c, lists: (c, 0)),
                pl.BlockSpec((total, BLK, width), lambda c, lists: (0, 0, 0), pipeline_mode=once),
                pl.BlockSpec((BLK, cand), lambda c, lists: (c, 0)),
            ],
            out_specs=[
                pl.BlockSpec((BLK, heads, width), lambda c, lists: (c, 0, 0)),
                pl.BlockSpec((BLK, heads), lambda c, lists: (c, 0)),
                pl.BlockSpec((total, BLK, width), lambda c, lists: (0, 0, 0), pipeline_mode=once),
            ],
            scratch_shapes=[
                pltpu.VMEM((cand, width), jnp.bfloat16),
                pltpu.VMEM((width, cand), jnp.bfloat16),
                pltpu.VMEM((BLK * heads, cand), jnp.bfloat16),
                pltpu.VMEM((BLK, heads, width), jnp.float32),
                pltpu.VMEM((BLK, cand), jnp.float32),
                pltpu.VMEM((BLK, cand), jnp.float32),
                pltpu.VMEM((width, cand), jnp.float32),
            ],
        ),
        out_shape=[
            jax.ShapeDtypeStruct(queries.shape, jnp.bfloat16),
            jax.ShapeDtypeStruct(head_weights.shape, jnp.float32),
            jax.ShapeDtypeStruct((total, BLK, width), jnp.float32),
        ],
        compiler_params=pltpu.CompilerParams(vmem_limit_bytes=60 * 2**20),
        cost_estimate=pl.CostEstimate(flops=flops, bytes_accessed=10 * 2**20, transcendentals=0),
    )(block_lists, queries, head_weights, table, targets)
    grad_keys = reduce_terms(grad_table.reshape((-1,) + keys.shape))
    return (grad_q, grad_w, grad_keys)


def solution(mesh):
    in_specs = (
        P(("groups", "ctx"), None, None),
        P(("groups", "ctx"), None),
        P(("groups", "ctx"), None),
        P(("groups", "ctx"), None),
        P(("groups", "ctx"), None),
    )
    out_specs = (
        P(("groups", "ctx"), None, None),
        P(("groups", "ctx"), None),
        P(("groups", "ctx"), None),
    )
    return jax.shard_map(shards, mesh=mesh, in_specs=in_specs, out_specs=out_specs, check_vma=False)
```

```python
import functools
import math

import jax
import jax.numpy as jnp
from jax import lax
from jax.experimental import pallas as pl
from jax.experimental.pallas import tpu as pltpu
from jax.sharding import PartitionSpec as P

BLK = 64
LOSS_WEIGHT = 256.0
FAR = 2**30
UC = 256
TF = 8
TB = 8


def compute_kernel(
    lists, q_ref, w_ref, table_ref, targets_ref, gq_ref, gw_ref, gk_ref,
    k_scr, kt_scr, s_scr, wb_scr, idx_scr, g_scr, gkt_scr, w_scr, gw_scr,
):
    c = pl.program_id(0)
    tokens, heads, width = q_ref.shape
    cand = targets_ref.shape[1]
    entries = cand // BLK
    inv_root = 1.0 / math.sqrt(width)

    @pl.when(c == 0)
    def _():
        gk_ref[...] = jnp.zeros_like(gk_ref)
        w_scr[...] = w_ref[...].T * inv_root

    for e in range(entries):
        source = jnp.maximum(lists[c, e], 0)
        k_scr[e * BLK : (e + 1) * BLK, :] = table_ref[source]
    kt_scr[...] = k_scr[...].T
    gkt_scr[...] = jnp.zeros_like(gkt_scr)

    for t0 in range(0, tokens, 8):
        wb_scr[t0 : t0 + 8] = jnp.broadcast_to(
            w_scr[pl.ds(c * tokens + t0, 8), :][:, :, None], (8, heads, width)
        )

    def forward(i, carry):
        t0 = pl.multiple_of(i * TF, TF)
        q = q_ref[pl.ds(t0, TF)].reshape(TF * heads, width)
        for u in range(0, cand, UC):
            s = jnp.dot(q, kt_scr[:, u : u + UC], preferred_element_type=jnp.float32)
            s_scr[pl.ds(t0 * heads, TF * heads), u : u + UC] = s.astype(jnp.bfloat16)
            s = jnp.maximum(s, 0.0).reshape(TF, heads, UC)
            parts = [
                jnp.sum(wb_scr[pl.ds(t0, TF)] * s[:, :, v : v + width], axis=1)
                for v in range(0, UC, width)
            ]
            idx_scr[pl.ds(t0, TF), u : u + UC] = jnp.concatenate(parts, axis=1)
        return carry

    lax.fori_loop(0, tokens // TF, forward, 0)

    lane = lax.broadcasted_iota(jnp.int32, (1, 2 * BLK), 1)
    pieces = []
    for e in range(0, entries, 2):
        low = jnp.where(lists[c, e] >= 0, lists[c, e] * BLK, FAR)
        high = jnp.where(lists[c, e + 1] >= 0, lists[c, e + 1] * BLK - BLK, FAR)
        pieces.append(jnp.where(lane < BLK, low, high) + lane)
    key_pos = jnp.concatenate(pieces, axis=1)
    for t0 in range(0, tokens, 8):
        row = lax.broadcasted_iota(jnp.int32, (8, cand), 0) + (lists[c, 0] * BLK + t0)
        allowed = key_pos <= row
        logits = jnp.where(allowed, idx_scr[t0 : t0 + 8, :], -jnp.inf)
        peak = jnp.max(logits, axis=1, keepdims=True)
        raised = jnp.exp(logits - peak)
        masked = jnp.where(allowed, targets_ref[t0 : t0 + 8, :], 0.0)
        p_scale = LOSS_WEIGHT / jnp.sum(raised, axis=1, keepdims=True)
        t_scale = LOSS_WEIGHT / jnp.sum(masked, axis=1, keepdims=True)
        g_scr[t0 : t0 + 8, :] = raised * p_scale - masked * t_scale

    def backward(i, carry):
        t0 = pl.multiple_of(i * TB, TB)
        rows = TB * heads
        q = q_ref[pl.ds(t0, TB)].astype(jnp.float32)
        wb = wb_scr[pl.ds(t0, TB)]
        wqt = (q * wb).reshape(rows, width).T.astype(jnp.bfloat16)
        gq = jnp.zeros((rows, width), jnp.float32)
        for u in range(0, cand, UC):
            g = g_scr[pl.ds(t0, TB), u : u + UC]
            g = jnp.broadcast_to(g[:, None, :], (TB, 16, UC)).astype(jnp.bfloat16)
            s = s_scr[pl.ds(t0 * heads, rows), u : u + UC].reshape(TB, heads // 16, 16, UC)
            mixed = jnp.where(s > 0, g[:, None], jnp.zeros((), jnp.bfloat16)).reshape(rows, UC)
            gq = gq + jnp.dot(
                mixed, k_scr[u : u + UC, :], preferred_element_type=jnp.float32
            )
            gkt_scr[:, u : u + UC] += jnp.dot(
                wqt, mixed, preferred_element_type=jnp.float32
            )
        gq = gq.reshape(TB, heads, width)
        gq_ref[pl.ds(t0, TB)] = (gq * wb).astype(jnp.bfloat16)
        gw_scr[pl.ds(c * tokens + t0, TB), :] = jnp.sum(gq * q, axis=2) * inv_root
        return carry

    lax.fori_loop(0, tokens // TB, backward, 0)

    for u in range(0, cand, 2 * BLK):
        part = gkt_scr[:, u : u + 2 * BLK].T
        for v in range(2):
            target = jnp.maximum(lists[c, u // BLK + v], 0)
            gk_ref[target] += part[v * BLK : (v + 1) * BLK, :]

    @pl.when(c == pl.num_programs(0) - 1)
    def _():
        gw_ref[...] = gw_scr[...].T


def axis_bits(count):
    return count.bit_length() - 1


def relative(me, r, bits):
    where = me
    for b in range(bits):
        if (r >> b) & 1:
            where = where + (1 - 2 * ((me // 2**b) % 2)) * 2**b
    return where


def low_bit(r, bits):
    return bits if r == 0 else (r & -r).bit_length() - 1


def greet(me, bits):
    barrier = pltpu.get_barrier_semaphore()
    for b in range(bits):
        pl.semaphore_signal(
            barrier,
            inc=1,
            device_id={"ctx": relative(me, 2**b, bits)},
            device_id_type=pl.DeviceIdType.MESH,
        )
    pl.semaphore_wait(barrier, bits)


def gather_kernel(count, keys_ref, all_ref, send_sem, recv_sem, own_sem):
    me = lax.axis_index("ctx")
    bits = axis_bits(count)
    own = pltpu.make_async_copy(keys_ref, all_ref.at[me], own_sem)
    own.start()
    greet(me, bits)

    def hop(r, b):
        where = relative(me, r, bits)
        return pltpu.make_async_remote_copy(
            src_ref=keys_ref if r == 0 else all_ref.at[where],
            dst_ref=all_ref.at[where],
            send_sem=send_sem.at[r + 2**b],
            recv_sem=recv_sem.at[r + 2**b],
            device_id={"ctx": relative(me, 2**b, bits)},
            device_id_type=pl.DeviceIdType.MESH,
        )

    def landed(r):
        where = relative(me, r, bits)
        return pltpu.make_async_remote_copy(
            src_ref=all_ref.at[where],
            dst_ref=all_ref.at[where],
            send_sem=send_sem.at[r],
            recv_sem=recv_sem.at[r],
            device_id={"ctx": relative(me, 2 ** low_bit(r, bits), bits)},
            device_id_type=pl.DeviceIdType.MESH,
        )

    sent = []
    for b in reversed(range(bits)):
        sent.append(hop(0, b))
        sent[-1].start()
    order = sorted(range(1, count), key=lambda r: (bin(r).count("1"), -low_bit(r, bits)))
    for r in order:
        landed(r).wait_recv()
        for b in reversed(range(low_bit(r, bits))):
            sent.append(hop(r, b))
            sent[-1].start()
    own.wait()
    for copy in sent:
        copy.wait_send()


def reduce_kernel(count, terms_ref, out_ref, send_buf, wide_buf, recv_buf, send_sem, recv_sem):
    me = lax.axis_index("ctx")
    bits = axis_bits(count)
    greet(me, bits)

    def hop(r):
        b = low_bit(r, bits)
        if b == 0:
            src, dst = terms_ref.at[relative(me, r, bits)], wide_buf.at[r // 2]
        else:
            src, dst = send_buf.at[r // 2], recv_buf.at[r // 2]
        return pltpu.make_async_remote_copy(
            src_ref=src,
            dst_ref=dst,
            send_sem=send_sem.at[r],
            recv_sem=recv_sem.at[r],
            device_id={"ctx": relative(me, 2**b, bits)},
            device_id_type=pl.DeviceIdType.MESH,
        )

    def total(r):
        value = terms_ref[relative(me, r, bits)]
        for b in range(low_bit(r, bits)):
            hop(r + 2**b).wait_recv()
            if b == 0:
                value = value + wide_buf[r // 2]
            else:
                value = value + recv_buf[(r + 2**b) // 2].astype(jnp.float32)
        return value

    def rank(r):
        b = low_bit(r, bits)
        return (b, low_bit(r - 2**b, bits), -r)

    order = sorted(range(1, count), key=rank)
    for r in order:
        if low_bit(r, bits) > 0:
            send_buf[r // 2] = total(r).astype(jnp.bfloat16)
        hop(r).start()
    out_ref[...] = total(0).astype(jnp.bfloat16)
    for r in order:
        hop(r).wait_send()


def gather_keys(keys):
    count = lax.axis_size("ctx")
    return pl.pallas_call(
        functools.partial(gather_kernel, count),
        out_shape=jax.ShapeDtypeStruct((count,) + keys.shape, keys.dtype),
        in_specs=[pl.BlockSpec(memory_space=pltpu.HBM)],
        out_specs=pl.BlockSpec(memory_space=pltpu.HBM),
        scratch_shapes=[
            pltpu.SemaphoreType.DMA((count,)),
            pltpu.SemaphoreType.DMA((count,)),
            pltpu.SemaphoreType.DMA,
        ],
        compiler_params=pltpu.CompilerParams(
            collective_id=0, has_side_effects=True, vmem_limit_bytes=32 * 2**20
        ),
    )(keys)


def reduce_terms(terms):
    count, rows, width = terms.shape
    return pl.pallas_call(
        functools.partial(reduce_kernel, count),
        out_shape=jax.ShapeDtypeStruct((rows, width), jnp.bfloat16),
        in_specs=[pl.BlockSpec(memory_space=pltpu.VMEM)],
        out_specs=pl.BlockSpec(memory_space=pltpu.VMEM),
        scratch_shapes=[
            pltpu.VMEM((count // 2, rows, width), jnp.bfloat16),
            pltpu.VMEM((count // 2, rows, width), jnp.float32),
            pltpu.VMEM((count // 2, rows, width), jnp.bfloat16),
            pltpu.SemaphoreType.DMA((count,)),
            pltpu.SemaphoreType.DMA((count,)),
        ],
        compiler_params=pltpu.CompilerParams(
            collective_id=1, has_side_effects=True, vmem_limit_bytes=52 * 2**20
        ),
    )(terms)


def local_grads(queries, head_weights, table, targets, block_lists):
    rows, heads, width = queries.shape
    cand = targets.shape[1]
    total = table.shape[0]
    flops = 6 * rows * heads * cand * width
    once = pl.Buffered(1)
    return pl.pallas_call(
        compute_kernel,
        grid_spec=pltpu.PrefetchScalarGridSpec(
            num_scalar_prefetch=1,
            grid=(block_lists.shape[0],),
            in_specs=[
                pl.BlockSpec((BLK, heads, width), lambda c, lists: (c, 0, 0)),
                pl.BlockSpec((heads, rows), lambda c, lists: (0, 0)),
                pl.BlockSpec((total, BLK, width), lambda c, lists: (0, 0, 0), pipeline_mode=once),
                pl.BlockSpec((BLK, cand), lambda c, lists: (c, 0)),
            ],
            out_specs=[
                pl.BlockSpec((BLK, heads, width), lambda c, lists: (c, 0, 0)),
                pl.BlockSpec((heads, rows), lambda c, lists: (0, 0)),
                pl.BlockSpec((total, BLK, width), lambda c, lists: (0, 0, 0), pipeline_mode=once),
            ],
            scratch_shapes=[
                pltpu.VMEM((cand, width), jnp.bfloat16),
                pltpu.VMEM((width, cand), jnp.bfloat16),
                pltpu.VMEM((BLK * heads, cand), jnp.bfloat16),
                pltpu.VMEM((BLK, heads, width), jnp.float32),
                pltpu.VMEM((BLK, cand), jnp.float32),
                pltpu.VMEM((BLK, cand), jnp.float32),
                pltpu.VMEM((width, cand), jnp.float32),
                pltpu.VMEM((rows, heads), jnp.float32),
                pltpu.VMEM((rows, heads), jnp.float32),
            ],
        ),
        out_shape=[
            jax.ShapeDtypeStruct(queries.shape, jnp.bfloat16),
            jax.ShapeDtypeStruct((heads, rows), jnp.float32),
            jax.ShapeDtypeStruct((total, BLK, width), jnp.float32),
        ],
        compiler_params=pltpu.CompilerParams(vmem_limit_bytes=60 * 2**20),
        cost_estimate=pl.CostEstimate(flops=flops, bytes_accessed=10 * 2**20, transcendentals=0),
    )(block_lists, queries, head_weights.T, table, targets)


def shards(queries, head_weights, keys, targets, block_lists):
    table = gather_keys(keys).reshape(-1, BLK, keys.shape[1])
    grad_q, grad_w, grad_table = local_grads(queries, head_weights, table, targets, block_lists)
    grad_keys = reduce_terms(grad_table.reshape((-1,) + keys.shape))
    return (grad_q, grad_w.T, grad_keys)


def solution(mesh):
    in_specs = (
        P(("groups", "ctx"), None, None),
        P(("groups", "ctx"), None),
        P(("groups", "ctx"), None),
        P(("groups", "ctx"), None),
        P(("groups", "ctx"), None),
    )
    out_specs = (
        P(("groups", "ctx"), None, None),
        P(("groups", "ctx"), None),
        P(("groups", "ctx"), None),
    )
    return jax.shard_map(shards, mesh=mesh, in_specs=in_specs, out_specs=out_specs, check_vma=False)
```

```python
import functools
import math

import jax
import jax.numpy as jnp
from jax import lax
from jax.experimental import pallas as pl
from jax.experimental.pallas import tpu as pltpu
from jax.sharding import PartitionSpec as P

BLK = 64
LOSS_WEIGHT = 256.0
FAR = 2**30
UC = 512
TF = 16
TB = 16


def compute_kernel(
    lists, q_ref, w_ref, table_ref, targets_ref, gq_ref, gw_ref, gk_ref,
    k_scr, kt_scr, s_scr, wb_scr, idx_scr, g_scr, gkt_scr, w_scr, gw_scr,
):
    c = pl.program_id(0)
    tokens, heads, width = q_ref.shape
    cand = targets_ref.shape[1]
    entries = cand // BLK
    inv_root = 1.0 / math.sqrt(width)

    @pl.when(c == 0)
    def _():
        gk_ref[...] = jnp.zeros_like(gk_ref)
        w_scr[...] = w_ref[...].T * inv_root

    for e in range(entries):
        source = jnp.maximum(lists[c, e], 0)
        k_scr[e * BLK : (e + 1) * BLK, :] = table_ref[source]
    kt_scr[...] = k_scr[...].T
    gkt_scr[...] = jnp.zeros_like(gkt_scr)

    for t0 in range(0, tokens, 8):
        wb_scr[t0 : t0 + 8] = jnp.broadcast_to(
            w_scr[pl.ds(c * tokens + t0, 8), :][:, :, None], (8, heads, width)
        )

    def forward(i, carry):
        t0 = pl.multiple_of(i * TF, TF)
        q = q_ref[pl.ds(t0, TF)].reshape(TF * heads, width)
        for u in range(0, cand, UC):
            s = jnp.dot(q, kt_scr[:, u : u + UC], preferred_element_type=jnp.float32)
            s_scr[pl.ds(t0 * heads, TF * heads), u : u + UC] = s.astype(jnp.bfloat16)
            s = jnp.maximum(s, 0.0).reshape(TF, heads, UC)
            parts = [
                jnp.sum(wb_scr[pl.ds(t0, TF)] * s[:, :, v : v + width], axis=1)
                for v in range(0, UC, width)
            ]
            idx_scr[pl.ds(t0, TF), u : u + UC] = jnp.concatenate(parts, axis=1)
        return carry

    lax.fori_loop(0, tokens // TF, forward, 0)

    lane = lax.broadcasted_iota(jnp.int32, (1, 2 * BLK), 1)
    pieces = []
    for e in range(0, entries, 2):
        low = jnp.where(lists[c, e] >= 0, lists[c, e] * BLK, FAR)
        high = jnp.where(lists[c, e + 1] >= 0, lists[c, e + 1] * BLK - BLK, FAR)
        pieces.append(jnp.where(lane < BLK, low, high) + lane)
    key_pos = jnp.concatenate(pieces, axis=1)
    for t0 in range(0, tokens, 8):
        row = lax.broadcasted_iota(jnp.int32, (8, cand), 0) + (lists[c, 0] * BLK + t0)
        allowed = key_pos <= row
        logits = jnp.where(allowed, idx_scr[t0 : t0 + 8, :], -jnp.inf)
        peak = jnp.max(logits, axis=1, keepdims=True)
        raised = jnp.exp(logits - peak)
        masked = jnp.where(allowed, targets_ref[t0 : t0 + 8, :], 0.0)
        p_scale = LOSS_WEIGHT / jnp.sum(raised, axis=1, keepdims=True)
        t_scale = LOSS_WEIGHT / jnp.sum(masked, axis=1, keepdims=True)
        g_scr[t0 : t0 + 8, :] = raised * p_scale - masked * t_scale

    def backward(i, carry):
        t0 = pl.multiple_of(i * TB, TB)
        rows = TB * heads
        q = q_ref[pl.ds(t0, TB)].astype(jnp.float32)
        wb = wb_scr[pl.ds(t0, TB)]
        wqt = (q * wb).reshape(rows, width).T.astype(jnp.bfloat16)
        gq = jnp.zeros((rows, width), jnp.float32)
        for u in range(0, cand, UC):
            g = g_scr[pl.ds(t0, TB), u : u + UC]
            g = jnp.broadcast_to(g[:, None, :], (TB, 16, UC)).astype(jnp.bfloat16)
            s = s_scr[pl.ds(t0 * heads, rows), u : u + UC].reshape(TB, heads // 16, 16, UC)
            mixed = jnp.where(s > 0, g[:, None], jnp.zeros((), jnp.bfloat16)).reshape(rows, UC)
            gq = gq + jnp.dot(
                mixed, k_scr[u : u + UC, :], preferred_element_type=jnp.float32
            )
            gkt_scr[:, u : u + UC] += jnp.dot(
                wqt, mixed, preferred_element_type=jnp.float32
            )
        gq = gq.reshape(TB, heads, width)
        gq_ref[pl.ds(t0, TB)] = (gq * wb).astype(jnp.bfloat16)
        gw_scr[pl.ds(c * tokens + t0, TB), :] = jnp.sum(gq * q, axis=2) * inv_root
        return carry

    lax.fori_loop(0, tokens // TB, backward, 0)

    for u in range(0, cand, 2 * BLK):
        part = gkt_scr[:, u : u + 2 * BLK].T
        for v in range(2):
            target = jnp.maximum(lists[c, u // BLK + v], 0)
            gk_ref[target] += part[v * BLK : (v + 1) * BLK, :]

    @pl.when(c == pl.num_programs(0) - 1)
    def _():
        gw_ref[...] = gw_scr[...].T


def axis_bits(count):
    return count.bit_length() - 1


def relative(me, r, bits):
    where = me
    for b in range(bits):
        if (r >> b) & 1:
            where = where + (1 - 2 * ((me // 2**b) % 2)) * 2**b
    return where


def low_bit(r, bits):
    return bits if r == 0 else (r & -r).bit_length() - 1


def greet(me, bits):
    barrier = pltpu.get_barrier_semaphore()
    for b in range(bits):
        pl.semaphore_signal(
            barrier,
            inc=1,
            device_id={"ctx": relative(me, 2**b, bits)},
            device_id_type=pl.DeviceIdType.MESH,
        )
    pl.semaphore_wait(barrier, bits)


def gather_kernel(count, keys_ref, all_ref, send_sem, recv_sem, own_sem):
    me = lax.axis_index("ctx")
    bits = axis_bits(count)
    own = pltpu.make_async_copy(keys_ref, all_ref.at[me], own_sem)
    own.start()
    greet(me, bits)

    def hop(r, b):
        where = relative(me, r, bits)
        return pltpu.make_async_remote_copy(
            src_ref=keys_ref if r == 0 else all_ref.at[where],
            dst_ref=all_ref.at[where],
            send_sem=send_sem.at[r + 2**b],
            recv_sem=recv_sem.at[r + 2**b],
            device_id={"ctx": relative(me, 2**b, bits)},
            device_id_type=pl.DeviceIdType.MESH,
        )

    def landed(r):
        where = relative(me, r, bits)
        return pltpu.make_async_remote_copy(
            src_ref=all_ref.at[where],
            dst_ref=all_ref.at[where],
            send_sem=send_sem.at[r],
            recv_sem=recv_sem.at[r],
            device_id={"ctx": relative(me, 2 ** low_bit(r, bits), bits)},
            device_id_type=pl.DeviceIdType.MESH,
        )

    sent = []
    for b in reversed(range(bits)):
        sent.append(hop(0, b))
        sent[-1].start()
    order = sorted(range(1, count), key=lambda r: (bin(r).count("1"), -low_bit(r, bits)))
    for r in order:
        landed(r).wait_recv()
        for b in reversed(range(low_bit(r, bits))):
            sent.append(hop(r, b))
            sent[-1].start()
    own.wait()
    for copy in sent:
        copy.wait_send()


def reduce_kernel(count, terms_ref, out_ref, send_buf, wide_buf, recv_buf, send_sem, recv_sem):
    me = lax.axis_index("ctx")
    bits = axis_bits(count)
    greet(me, bits)

    def hop(r):
        b = low_bit(r, bits)
        if b == 0:
            src, dst = terms_ref.at[relative(me, r, bits)], wide_buf.at[r // 2]
        else:
            src, dst = send_buf.at[r // 2], recv_buf.at[r // 2]
        return pltpu.make_async_remote_copy(
            src_ref=src,
            dst_ref=dst,
            send_sem=send_sem.at[r],
            recv_sem=recv_sem.at[r],
            device_id={"ctx": relative(me, 2**b, bits)},
            device_id_type=pl.DeviceIdType.MESH,
        )

    def total(r):
        value = terms_ref[relative(me, r, bits)]
        for b in range(low_bit(r, bits)):
            hop(r + 2**b).wait_recv()
            if b == 0:
                value = value + wide_buf[r // 2]
            else:
                value = value + recv_buf[(r + 2**b) // 2].astype(jnp.float32)
        return value

    def rank(r):
        b = low_bit(r, bits)
        return (b, low_bit(r - 2**b, bits), -r)

    order = sorted(range(1, count), key=rank)
    for r in order:
        if low_bit(r, bits) > 0:
            send_buf[r // 2] = total(r).astype(jnp.bfloat16)
        hop(r).start()
    out_ref[...] = total(0).astype(jnp.bfloat16)
    for r in order:
        hop(r).wait_send()


def gather_keys(keys):
    count = lax.axis_size("ctx")
    return pl.pallas_call(
        functools.partial(gather_kernel, count),
        out_shape=jax.ShapeDtypeStruct((count,) + keys.shape, keys.dtype),
        in_specs=[pl.BlockSpec(memory_space=pltpu.HBM)],
        out_specs=pl.BlockSpec(memory_space=pltpu.HBM),
        scratch_shapes=[
            pltpu.SemaphoreType.DMA((count,)),
            pltpu.SemaphoreType.DMA((count,)),
            pltpu.SemaphoreType.DMA,
        ],
        compiler_params=pltpu.CompilerParams(
            collective_id=0, has_side_effects=True, vmem_limit_bytes=32 * 2**20
        ),
    )(keys)


def reduce_terms(terms):
    count, rows, width = terms.shape
    return pl.pallas_call(
        functools.partial(reduce_kernel, count),
        out_shape=jax.ShapeDtypeStruct((rows, width), jnp.bfloat16),
        in_specs=[pl.BlockSpec(memory_space=pltpu.VMEM)],
        out_specs=pl.BlockSpec(memory_space=pltpu.VMEM),
        scratch_shapes=[
            pltpu.VMEM((count // 2, rows, width), jnp.bfloat16),
            pltpu.VMEM((count // 2, rows, width), jnp.float32),
            pltpu.VMEM((count // 2, rows, width), jnp.bfloat16),
            pltpu.SemaphoreType.DMA((count,)),
            pltpu.SemaphoreType.DMA((count,)),
        ],
        compiler_params=pltpu.CompilerParams(
            collective_id=1, has_side_effects=True, vmem_limit_bytes=52 * 2**20
        ),
    )(terms)


def local_grads(queries, head_weights, table, targets, block_lists):
    rows, heads, width = queries.shape
    cand = targets.shape[1]
    total = table.shape[0]
    flops = 6 * rows * heads * cand * width
    once = pl.Buffered(1)
    return pl.pallas_call(
        compute_kernel,
        grid_spec=pltpu.PrefetchScalarGridSpec(
            num_scalar_prefetch=1,
            grid=(block_lists.shape[0],),
            in_specs=[
                pl.BlockSpec((BLK, heads, width), lambda c, lists: (c, 0, 0)),
                pl.BlockSpec((heads, rows), lambda c, lists: (0, 0)),
                pl.BlockSpec((total, BLK, width), lambda c, lists: (0, 0, 0), pipeline_mode=once),
                pl.BlockSpec((BLK, cand), lambda c, lists: (c, 0)),
            ],
            out_specs=[
                pl.BlockSpec((BLK, heads, width), lambda c, lists: (c, 0, 0)),
                pl.BlockSpec((heads, rows), lambda c, lists: (0, 0)),
                pl.BlockSpec((total, BLK, width), lambda c, lists: (0, 0, 0), pipeline_mode=once),
            ],
            scratch_shapes=[
                pltpu.VMEM((cand, width), jnp.bfloat16),
                pltpu.VMEM((width, cand), jnp.bfloat16),
                pltpu.VMEM((BLK * heads, cand), jnp.bfloat16),
                pltpu.VMEM((BLK, heads, width), jnp.float32),
                pltpu.VMEM((BLK, cand), jnp.float32),
                pltpu.VMEM((BLK, cand), jnp.float32),
                pltpu.VMEM((width, cand), jnp.float32),
                pltpu.VMEM((rows, heads), jnp.float32),
                pltpu.VMEM((rows, heads), jnp.float32),
            ],
        ),
        out_shape=[
            jax.ShapeDtypeStruct(queries.shape, jnp.bfloat16),
            jax.ShapeDtypeStruct((heads, rows), jnp.float32),
            jax.ShapeDtypeStruct((total, BLK, width), jnp.float32),
        ],
        compiler_params=pltpu.CompilerParams(vmem_limit_bytes=60 * 2**20),
        cost_estimate=pl.CostEstimate(flops=flops, bytes_accessed=10 * 2**20, transcendentals=0),
    )(block_lists, queries, head_weights.T, table, targets)


def shards(queries, head_weights, keys, targets, block_lists):
    table = gather_keys(keys).reshape(-1, BLK, keys.shape[1])
    grad_q, grad_w, grad_table = local_grads(queries, head_weights, table, targets, block_lists)
    grad_keys = reduce_terms(grad_table.reshape((-1,) + keys.shape))
    return (grad_q, grad_w.T, grad_keys)


def solution(mesh):
    in_specs = (
        P(("groups", "ctx"), None, None),
        P(("groups", "ctx"), None),
        P(("groups", "ctx"), None),
        P(("groups", "ctx"), None),
        P(("groups", "ctx"), None),
    )
    out_specs = (
        P(("groups", "ctx"), None, None),
        P(("groups", "ctx"), None),
        P(("groups", "ctx"), None),
    )
    return jax.shard_map(shards, mesh=mesh, in_specs=in_specs, out_specs=out_specs, check_vma=False)
```

```python
import functools
import math

import jax
import jax.numpy as jnp
from jax import lax
from jax.experimental import pallas as pl
from jax.experimental.pallas import tpu as pltpu
from jax.sharding import PartitionSpec as P

BLK = 64
LOSS_WEIGHT = 256.0
FAR = 2**30
UC = 256
TF = 32
TB = 32


def compute_kernel(
    lists, q_ref, w_ref, table_ref, targets_ref, gq_ref, gw_ref, gk_ref,
    k_scr, kt_scr, s_scr, wb_scr, idx_scr, g_scr, gkt_scr, w_scr, gw_scr,
):
    c = pl.program_id(0)
    tokens, heads, width = q_ref.shape
    cand = targets_ref.shape[1]
    entries = cand // BLK
    inv_root = 1.0 / math.sqrt(width)

    @pl.when(c == 0)
    def _():
        gk_ref[...] = jnp.zeros_like(gk_ref)
        w_scr[...] = w_ref[...].T * inv_root

    for e in range(entries):
        source = jnp.maximum(lists[c, e], 0)
        k_scr[e * BLK : (e + 1) * BLK, :] = table_ref[source]
    kt_scr[...] = k_scr[...].T
    gkt_scr[...] = jnp.zeros_like(gkt_scr)

    for t0 in range(0, tokens, 8):
        wb_scr[t0 : t0 + 8] = jnp.broadcast_to(
            w_scr[pl.ds(c * tokens + t0, 8), :][:, :, None], (8, heads, width)
        )

    def forward(i, carry):
        t0 = pl.multiple_of(i * TF, TF)
        q = q_ref[pl.ds(t0, TF)].reshape(TF * heads, width)
        for u in range(0, cand, UC):
            s = jnp.dot(q, kt_scr[:, u : u + UC], preferred_element_type=jnp.float32)
            s_scr[pl.ds(t0 * heads, TF * heads), u : u + UC] = s.astype(jnp.bfloat16)
            s = jnp.maximum(s, 0.0).reshape(TF, heads, UC)
            parts = [
                jnp.sum(wb_scr[pl.ds(t0, TF)] * s[:, :, v : v + width], axis=1)
                for v in range(0, UC, width)
            ]
            idx_scr[pl.ds(t0, TF), u : u + UC] = jnp.concatenate(parts, axis=1)
        return carry

    lax.fori_loop(0, tokens // TF, forward, 0)

    lane = lax.broadcasted_iota(jnp.int32, (1, 2 * BLK), 1)
    pieces = []
    for e in range(0, entries, 2):
        low = jnp.where(lists[c, e] >= 0, lists[c, e] * BLK, FAR)
        high = jnp.where(lists[c, e + 1] >= 0, lists[c, e + 1] * BLK - BLK, FAR)
        pieces.append(jnp.where(lane < BLK, low, high) + lane)
    key_pos = jnp.concatenate(pieces, axis=1)
    for t0 in range(0, tokens, 8):
        row = lax.broadcasted_iota(jnp.int32, (8, cand), 0) + (lists[c, 0] * BLK + t0)
        allowed = key_pos <= row
        logits = jnp.where(allowed, idx_scr[t0 : t0 + 8, :], -jnp.inf)
        peak = jnp.max(logits, axis=1, keepdims=True)
        raised = jnp.exp(logits - peak)
        masked = jnp.where(allowed, targets_ref[t0 : t0 + 8, :], 0.0)
        p_scale = LOSS_WEIGHT / jnp.sum(raised, axis=1, keepdims=True)
        t_scale = LOSS_WEIGHT / jnp.sum(masked, axis=1, keepdims=True)
        g_scr[t0 : t0 + 8, :] = raised * p_scale - masked * t_scale

    def backward(i, carry):
        t0 = pl.multiple_of(i * TB, TB)
        rows = TB * heads
        q = q_ref[pl.ds(t0, TB)].astype(jnp.float32)
        wb = wb_scr[pl.ds(t0, TB)]
        wqt = (q * wb).reshape(rows, width).T.astype(jnp.bfloat16)
        gq = jnp.zeros((rows, width), jnp.float32)
        for u in range(0, cand, UC):
            g = g_scr[pl.ds(t0, TB), u : u + UC]
            g = jnp.broadcast_to(g[:, None, :], (TB, 16, UC)).astype(jnp.bfloat16)
            s = s_scr[pl.ds(t0 * heads, rows), u : u + UC].reshape(TB, heads // 16, 16, UC)
            mixed = jnp.where(s > 0, g[:, None], jnp.zeros((), jnp.bfloat16)).reshape(rows, UC)
            gq = gq + jnp.dot(
                mixed, k_scr[u : u + UC, :], preferred_element_type=jnp.float32
            )
            gkt_scr[:, u : u + UC] += jnp.dot(
                wqt, mixed, preferred_element_type=jnp.float32
            )
        gq = gq.reshape(TB, heads, width)
        gq_ref[pl.ds(t0, TB)] = (gq * wb).astype(jnp.bfloat16)
        gw_scr[pl.ds(c * tokens + t0, TB), :] = jnp.sum(gq * q, axis=2) * inv_root
        return carry

    lax.fori_loop(0, tokens // TB, backward, 0)

    for u in range(0, cand, 2 * BLK):
        part = gkt_scr[:, u : u + 2 * BLK].T
        for v in range(2):
            target = jnp.maximum(lists[c, u // BLK + v], 0)
            gk_ref[target] += part[v * BLK : (v + 1) * BLK, :]

    @pl.when(c == pl.num_programs(0) - 1)
    def _():
        gw_ref[...] = gw_scr[...].T


def axis_bits(count):
    return count.bit_length() - 1


def relative(me, r, bits):
    where = me
    for b in range(bits):
        if (r >> b) & 1:
            where = where + (1 - 2 * ((me // 2**b) % 2)) * 2**b
    return where


def low_bit(r, bits):
    return bits if r == 0 else (r & -r).bit_length() - 1


def greet(me, bits):
    barrier = pltpu.get_barrier_semaphore()
    for b in range(bits):
        pl.semaphore_signal(
            barrier,
            inc=1,
            device_id={"ctx": relative(me, 2**b, bits)},
            device_id_type=pl.DeviceIdType.MESH,
        )
    pl.semaphore_wait(barrier, bits)


def gather_kernel(count, keys_ref, all_ref, send_sem, recv_sem, own_sem):
    me = lax.axis_index("ctx")
    bits = axis_bits(count)
    own = pltpu.make_async_copy(keys_ref, all_ref.at[me], own_sem)
    own.start()
    greet(me, bits)

    def hop(r, b):
        where = relative(me, r, bits)
        return pltpu.make_async_remote_copy(
            src_ref=keys_ref if r == 0 else all_ref.at[where],
            dst_ref=all_ref.at[where],
            send_sem=send_sem.at[r + 2**b],
            recv_sem=recv_sem.at[r + 2**b],
            device_id={"ctx": relative(me, 2**b, bits)},
            device_id_type=pl.DeviceIdType.MESH,
        )

    def landed(r):
        where = relative(me, r, bits)
        return pltpu.make_async_remote_copy(
            src_ref=all_ref.at[where],
            dst_ref=all_ref.at[where],
            send_sem=send_sem.at[r],
            recv_sem=recv_sem.at[r],
            device_id={"ctx": relative(me, 2 ** low_bit(r, bits), bits)},
            device_id_type=pl.DeviceIdType.MESH,
        )

    sent = []
    for b in reversed(range(bits)):
        sent.append(hop(0, b))
        sent[-1].start()
    order = sorted(range(1, count), key=lambda r: (bin(r).count("1"), -low_bit(r, bits)))
    for r in order:
        landed(r).wait_recv()
        for b in reversed(range(low_bit(r, bits))):
            sent.append(hop(r, b))
            sent[-1].start()
    own.wait()
    for copy in sent:
        copy.wait_send()


def reduce_kernel(count, terms_ref, out_ref, send_buf, wide_buf, recv_buf, send_sem, recv_sem):
    me = lax.axis_index("ctx")
    bits = axis_bits(count)
    greet(me, bits)

    def hop(r):
        b = low_bit(r, bits)
        if b == 0:
            src, dst = terms_ref.at[relative(me, r, bits)], wide_buf.at[r // 2]
        else:
            src, dst = send_buf.at[r // 2], recv_buf.at[r // 2]
        return pltpu.make_async_remote_copy(
            src_ref=src,
            dst_ref=dst,
            send_sem=send_sem.at[r],
            recv_sem=recv_sem.at[r],
            device_id={"ctx": relative(me, 2**b, bits)},
            device_id_type=pl.DeviceIdType.MESH,
        )

    def total(r):
        value = terms_ref[relative(me, r, bits)]
        for b in range(low_bit(r, bits)):
            hop(r + 2**b).wait_recv()
            if b == 0:
                value = value + wide_buf[r // 2]
            else:
                value = value + recv_buf[(r + 2**b) // 2].astype(jnp.float32)
        return value

    def rank(r):
        b = low_bit(r, bits)
        return (b, low_bit(r - 2**b, bits), -r)

    order = sorted(range(1, count), key=rank)
    for r in order:
        if low_bit(r, bits) > 0:
            send_buf[r // 2] = total(r).astype(jnp.bfloat16)
        hop(r).start()
    out_ref[...] = total(0).astype(jnp.bfloat16)
    for r in order:
        hop(r).wait_send()


def gather_keys(keys):
    count = lax.axis_size("ctx")
    return pl.pallas_call(
        functools.partial(gather_kernel, count),
        out_shape=jax.ShapeDtypeStruct((count,) + keys.shape, keys.dtype),
        in_specs=[pl.BlockSpec(memory_space=pltpu.HBM)],
        out_specs=pl.BlockSpec(memory_space=pltpu.HBM),
        scratch_shapes=[
            pltpu.SemaphoreType.DMA((count,)),
            pltpu.SemaphoreType.DMA((count,)),
            pltpu.SemaphoreType.DMA,
        ],
        compiler_params=pltpu.CompilerParams(
            collective_id=0, has_side_effects=True, vmem_limit_bytes=32 * 2**20
        ),
    )(keys)


def reduce_terms(terms):
    count, rows, width = terms.shape
    return pl.pallas_call(
        functools.partial(reduce_kernel, count),
        out_shape=jax.ShapeDtypeStruct((rows, width), jnp.bfloat16),
        in_specs=[pl.BlockSpec(memory_space=pltpu.VMEM)],
        out_specs=pl.BlockSpec(memory_space=pltpu.VMEM),
        scratch_shapes=[
            pltpu.VMEM((count // 2, rows, width), jnp.bfloat16),
            pltpu.VMEM((count // 2, rows, width), jnp.float32),
            pltpu.VMEM((count // 2, rows, width), jnp.bfloat16),
            pltpu.SemaphoreType.DMA((count,)),
            pltpu.SemaphoreType.DMA((count,)),
        ],
        compiler_params=pltpu.CompilerParams(
            collective_id=1, has_side_effects=True, vmem_limit_bytes=52 * 2**20
        ),
    )(terms)


def local_grads(queries, head_weights, table, targets, block_lists):
    rows, heads, width = queries.shape
    cand = targets.shape[1]
    total = table.shape[0]
    flops = 6 * rows * heads * cand * width
    once = pl.Buffered(1)
    return pl.pallas_call(
        compute_kernel,
        grid_spec=pltpu.PrefetchScalarGridSpec(
            num_scalar_prefetch=1,
            grid=(block_lists.shape[0],),
            in_specs=[
                pl.BlockSpec((BLK, heads, width), lambda c, lists: (c, 0, 0)),
                pl.BlockSpec((heads, rows), lambda c, lists: (0, 0)),
                pl.BlockSpec((total, BLK, width), lambda c, lists: (0, 0, 0), pipeline_mode=once),
                pl.BlockSpec((BLK, cand), lambda c, lists: (c, 0)),
            ],
            out_specs=[
                pl.BlockSpec((BLK, heads, width), lambda c, lists: (c, 0, 0)),
                pl.BlockSpec((heads, rows), lambda c, lists: (0, 0)),
                pl.BlockSpec((total, BLK, width), lambda c, lists: (0, 0, 0), pipeline_mode=once),
            ],
            scratch_shapes=[
                pltpu.VMEM((cand, width), jnp.bfloat16),
                pltpu.VMEM((width, cand), jnp.bfloat16),
                pltpu.VMEM((BLK * heads, cand), jnp.bfloat16),
                pltpu.VMEM((BLK, heads, width), jnp.float32),
                pltpu.VMEM((BLK, cand), jnp.float32),
                pltpu.VMEM((BLK, cand), jnp.float32),
                pltpu.VMEM((width, cand), jnp.float32),
                pltpu.VMEM((rows, heads), jnp.float32),
                pltpu.VMEM((rows, heads), jnp.float32),
            ],
        ),
        out_shape=[
            jax.ShapeDtypeStruct(queries.shape, jnp.bfloat16),
            jax.ShapeDtypeStruct((heads, rows), jnp.float32),
            jax.ShapeDtypeStruct((total, BLK, width), jnp.float32),
        ],
        compiler_params=pltpu.CompilerParams(vmem_limit_bytes=60 * 2**20),
        cost_estimate=pl.CostEstimate(flops=flops, bytes_accessed=10 * 2**20, transcendentals=0),
    )(block_lists, queries, head_weights.T, table, targets)


def shards(queries, head_weights, keys, targets, block_lists):
    table = gather_keys(keys).reshape(-1, BLK, keys.shape[1])
    grad_q, grad_w, grad_table = local_grads(queries, head_weights, table, targets, block_lists)
    grad_keys = reduce_terms(grad_table.reshape((-1,) + keys.shape))
    return (grad_q, grad_w.T, grad_keys)


def solution(mesh):
    in_specs = (
        P(("groups", "ctx"), None, None),
        P(("groups", "ctx"), None),
        P(("groups", "ctx"), None),
        P(("groups", "ctx"), None),
        P(("groups", "ctx"), None),
    )
    out_specs = (
        P(("groups", "ctx"), None, None),
        P(("groups", "ctx"), None),
        P(("groups", "ctx"), None),
    )
    return jax.shard_map(shards, mesh=mesh, in_specs=in_specs, out_specs=out_specs, check_vma=False)
```
